1024 devices in a mesh: sub: 128 (over z, y_lo, core), grp: 4 (over x), rep: 2 (over y_hi).
Axes of the slice: x: 4, y: 8 (y_hi: 2, y_lo: 4; y = y_hi * 4 + y_lo), z: 16, core: 2. Of those that a mesh axis runs over, the one named last changes fastest.
Arguments:
- residual: float32 [524288, 128], P(('sub', 'grp', 'rep'))
- direction: float32 [524288, 128], P(('sub', 'grp', 'rep'))
- sub_blocks: bfloat16 [16384, 4, 128, 128], P(('sub', 'grp', 'rep')), may hold values from -0.15625 to 0.15625
- pattern: int32 [16384, 4], P(('sub', 'grp', 'rep')), may hold values from 0 to 15
- facing_block_lookup: int32 [1024, 4], P(('sub', 'grp', 'rep')), may hold values from 0 to 3, each once within a row
- corners: int32 [1024, 8], P(('sub', 'grp', 'rep')), may hold values from 0 to 511, as said below
- coarse_inverse: float32 [8192, 8192], P(('sub', 'grp', 'rep')), as said below
Outputs:
- residual_new: float32 [524288, 128], P(('sub', 'grp', 'rep'))
- direction_new: float32 [524288, 128], P(('sub', 'grp', 'rep'))
The draws below stay inside these ranges and needn't reach their ends.
Inputs may be any that keep to these rules, and one draw needn't show every extreme that they name: `pattern`: block indices of the subdomain's own node blocks, repeats allowed. `facing_block_lookup`: each row is a permutation. `corners`: entry i of a row lies in i * 64 to (i + 1) * 64 - 1. `coarse_inverse`: symmetric.
All inputs are finite; a program needn't handle non-finite values.
Results may differ from the reference program's by a relative error of at most 0.002.
Values sent between devices are 32-bit elements; how exact they have to be, the bound alone decides.
A program may use at most 32 MiB of HBM per device.

```python
import math
import jax
import jax.numpy as jnp
from jax import lax

TRACKS = 128
ROWB = 16
BLK = 128
FB = 4
NNZ = 4
SWEEPS = 3
NCI = 8
NSUB = 1024
FACE = 512
NC = 8192


def field_pair(key):
    shape = (NSUB * FACE, TRACKS)
    node_scale = 0.3 * jnp.exp(math.log(10.0) * jax.random.uniform(jax.random.fold_in(key, 102), (NSUB * FACE, 1)))
    track_scale = 0.3 * jnp.exp(math.log(10.0) * jax.random.uniform(jax.random.fold_in(key, 103), (1, TRACKS)))
    block_position = (jnp.arange(NSUB * FACE) // FACE).astype(jnp.float32)[:, None] / max(NSUB - 1, 1)
    ramp = 0.6 * jnp.exp(math.log(3.0) * block_position)
    base = jax.random.truncated_normal(jax.random.fold_in(key, 101), -4.0, 4.0, shape)
    noise = jax.random.truncated_normal(jax.random.fold_in(key, 105), -4.0, 4.0, shape)
    scales = node_scale * track_scale * ramp
    return (base * scales, (base + 0.5 * noise) * scales)


def draw_residual(key, part):
    entry_values = field_pair(key)
    return entry_values[0].astype(jnp.float32)


def draw_direction(key, part):
    entry_values = field_pair(key)
    return entry_values[1].astype(jnp.float32)


def draw_corners(key, part):
    segment = FACE // NCI
    offsets = jax.random.randint(jax.random.fold_in(key, 301), (NSUB, NCI), 0, segment)
    starts = jnp.arange(NCI, dtype=jnp.int32)[None, :] * segment
    return (starts + offsets).astype(jnp.int32)


def draw_coarse_inverse(key, part):
    order = NC
    general = jax.random.truncated_normal(jax.random.fold_in(key, 201), -4.0, 4.0, (order, order))
    strong = jax.random.truncated_normal(jax.random.fold_in(key, 202), -4.0, 4.0, (order, order))
    general = (general + general.T) * (0.5 / math.sqrt(2.0 * order))
    strong = (strong + strong.T) * (0.3 / math.sqrt(2.0 * NCI))
    owners = jnp.arange(order, dtype=jnp.int32) // NCI
    count = order // NCI
    half = count // 2
    paired_next = jnp.bitwise_xor(owners[:, None], 1) == owners[None, :]
    partner_upper_blocks = (owners[:, None] + half) % count == owners[None, :]
    paired = jnp.logical_or(paired_next, partner_upper_blocks)
    diagonal = jax.random.uniform(jax.random.fold_in(key, 203), (order,), minval=0.5, maxval=1.5)
    on_diagonal = jnp.arange(order)[:, None] == jnp.arange(order)[None, :]
    entry_values = general + jnp.where(paired, strong, 0.0)
    entry_values = jnp.where(on_diagonal, diagonal[:, None] + jnp.zeros((order, order)), entry_values)
    return entry_values.astype(jnp.float32)


def plant(result, rng, low, largest):
    extent = result.shape
    index_at = [jax.random.randint(jax.random.fold_in(rng, axis), (), 0, extent[axis]) for axis in range(len(extent))]
    result = result.at[tuple(index_at)].set(low)
    longest = extent.index(max(extent))
    index_at[longest] = (index_at[longest] + 1) % extent[longest]
    return result.at[tuple(index_at)].set(largest)


def level_of(key, shape, pieces, least, high):
    def one(axis_at, parts):
        draws = jax.random.uniform(jax.random.fold_in(jax.random.fold_in(key, 6), axis_at), (parts,), jnp.float32, least / len(pieces), high / len(pieces))
        return jnp.repeat(jnp.exp(draws), shape[axis_at] // parts).reshape((-1,) + (1,) * (len(shape) - axis_at - 1))

    loudness = one(*pieces[0])
    for cut in pieces[1:]:
        loudness = loudness * one(*cut)
    return loudness


def gaussian(stream_key, shape, deviation, most, split=(), kind=jnp.bfloat16):
    array = deviation * jax.random.normal(stream_key, shape, jnp.float32)
    if split:
        array = array * level_of(stream_key, shape, split, -0.22, 0.18)
    return jnp.clip(array, -most, most).astype(kind)


def setup_inputs(seed: int = 0) -> dict:
    keys = jax.random.split(jax.random.key(seed), 8)
    residual = draw_residual(jax.random.fold_in(keys[7], 71), 0)
    direction = draw_direction(jax.random.fold_in(keys[7], 71), 0)
    sub_blocks = gaussian(keys[2], (NSUB * ROWB, NNZ, BLK, BLK), (3 * NNZ * BLK) ** -0.5, 0.15625, ((0, 1024),))
    pattern = plant(jax.random.randint(keys[3], (NSUB * ROWB, NNZ), 0, ROWB), jax.random.fold_in(keys[3], 1), 0, ROWB - 1).astype(jnp.int32)
    facing_block_lookup = jax.vmap(lambda own: jax.random.permutation(own, FB))(jax.random.split(keys[4], NSUB)).reshape((NSUB, FB)).astype(jnp.int32)
    corners = draw_corners(jax.random.fold_in(keys[7], 71), 0)
    coarse_inverse = draw_coarse_inverse(jax.random.fold_in(keys[7], 71), 0)
    return {"residual": residual, "direction": direction, "sub_blocks": sub_blocks, "pattern": pattern, "facing_block_lookup": facing_block_lookup, "corners": corners, "coarse_inverse": coarse_inverse}


def relax_one(sub_blocks, pattern, source):
    relaxed = source
    for sweep_index in range(SWEEPS):
        rounded = lax.optimization_barrier(relaxed.astype(jnp.bfloat16))
        picked = rounded[pattern].astype(jnp.float32)
        product = jnp.einsum("rkij,rkjt->rit", sub_blocks.astype(jnp.float32), picked)
        relaxed = source - product
    return relaxed


def reference(residual, direction, sub_blocks, pattern, facing_block_lookup, corners, coarse_inverse):
    local_subdomain_blocks = direction.reshape(NSUB, FB, BLK, TRACKS)
    moved = jnp.take_along_axis(local_subdomain_blocks, facing_block_lookup[:, :, None, None], axis=1)
    incoming = jnp.concatenate([jnp.zeros_like(moved[:1]), moved[:-1]], axis=0)
    interior = jnp.zeros((NSUB, ROWB - 2 * FB, BLK, TRACKS), dtype=jnp.float32)
    source = jnp.concatenate([-incoming, local_subdomain_blocks, interior], axis=1)
    group_size = math.gcd(NSUB, 16)
    group_count = NSUB // group_size
    blocks_grouped = sub_blocks.reshape(group_count, group_size, ROWB, NNZ, BLK, BLK)
    pattern_grouped = pattern.reshape(group_count, group_size, ROWB, NNZ)
    source_grouped = source.reshape(group_count, group_size, ROWB, BLK, TRACKS)

    def apply_group(items):
        return jax.vmap(relax_one)(items[0], items[1], items[2])

    relaxed = lax.map(apply_group, (blocks_grouped, pattern_grouped, source_grouped))
    relaxed = relaxed.reshape(NSUB, ROWB, BLK, TRACKS)
    upper = relaxed[:, FB:2 * FB]
    lower = relaxed[:, :FB]
    arriving = jnp.concatenate([lower[1:], jnp.zeros_like(lower[:1])], axis=0)
    rows_index = jnp.arange(NSUB, dtype=jnp.int32)[:, None]
    mapped = jnp.zeros_like(arriving).at[rows_index, facing_block_lookup].set(arriving)
    upper_flat = upper.reshape(NSUB, FACE, TRACKS)
    mapped_flat = mapped.reshape(NSUB, FACE, TRACKS)
    summed = upper_flat + mapped_flat
    jumped = upper_flat - mapped_flat
    corner_totals = jnp.take_along_axis(summed, corners[:, :, None], axis=1)
    coarse_part = jnp.dot(coarse_inverse, corner_totals.reshape(NC, TRACKS),
                          precision=lax.Precision.HIGHEST, preferred_element_type=jnp.float32)
    image = jumped.at[rows_index, corners].add(coarse_part.reshape(NSUB, NCI, TRACKS))
    image = image.reshape(NSUB * FACE, TRACKS)
    norm_old = jnp.sum(residual * residual, axis=0)
    cross = jnp.sum(residual * image, axis=0)
    curvature = jnp.sum(image * image, axis=0)
    residual_new = residual - (cross / curvature) * image
    norm_new = jnp.sum(residual_new * residual_new, axis=0)
    direction_new = residual_new + (norm_new / norm_old) * direction
    return residual_new, direction_new
```

```python
import functools

import jax
import jax.numpy as jnp
from jax import lax
from jax.experimental import pallas as pl
from jax.experimental.pallas import tpu as pltpu
from jax.sharding import PartitionSpec as P

MESH = pl.DeviceIdType.MESH
AXES = ("sub", "grp", "rep")
SWEEPS = 3
CORES = 2
LANES = 128


def two_sum(a, b):
    s = a + b
    t = s - a
    return s, (a - (s - t)) + (b - t)


def split(a):
    c = a * 4097.0
    hi = c - (c - a)
    return hi, a - hi


def two_product(a, b):
    p = a * b
    ah, al = split(a)
    bh, bl = split(b)
    return p, ((ah * bh - p) + ah * bl + al * bh) + al * bl


def pair_add(a, b):
    s, e = two_sum(a[0], b[0])
    return s, e + (a[1] + b[1])


def tidy(a):
    s = a[0] + a[1]
    return s, a[1] - (s - a[0])


def add_product(total, a, b):
    p, e = two_product(a, b)
    return pair_add(total, (p, e))


def fold(pair, axis=0):
    while pair[0].shape[axis] > 1:
        half = pair[0].shape[axis] // 2
        pair = pair_add(
            tuple(lax.slice_in_dim(v, 0, half, axis=axis) for v in pair),
            tuple(lax.slice_in_dim(v, half, 2 * half, axis=axis) for v in pair),
        )
    return pair


def kernel(
    sizes,
    pattern,
    facing,
    corners,
    residual_hbm,
    direction_hbm,
    blocks_hbm,
    coarse_hbm,
    image,
    factors,
    residual,
    direction,
    blocks,
    coarse,
    source,
    rounded,
    upper,
    forward_out,
    forward_in,
    back_out,
    back_in,
    corner_out,
    corner_in,
    packed,
    columns,
    turned,
    totals,
    part,
    part_in,
    sums_plane,
    sums_line,
    load_sem,
    forward_send,
    forward_recv,
    back_send,
    back_recv,
    corner_send,
    corner_recv,
    group_send,
    group_recv,
):
    n_z, n_yl, n_grp, n_rep = sizes
    n_line, n_plane = n_z * CORES, n_yl * n_grp * n_rep
    count = n_line * n_plane
    faces, block, tracks = forward_in.shape[0], direction.shape[1], direction.shape[2]
    row_blocks, nnz = blocks.shape[:2]
    n_corners = corners.shape[1]
    segment = faces * block // n_corners
    per_block = block // segment

    sub, grp, rep = (lax.axis_index(a) for a in AXES)
    k = (sub * n_grp + grp) * n_rep + rep
    core, yl, z = sub % CORES, (sub // CORES) % n_yl, sub // (CORES * n_yl)
    line = z * CORES + core
    plane = (yl * n_grp + grp) * n_rep + rep

    def device_of(index):
        return (index // (n_grp * n_rep), (index // n_rep) % n_grp, index % n_rep)

    def on_line(place):
        return ((place // CORES * n_yl + yl) * CORES + place % CORES, grp, rep)

    def on_plane(place):
        there = (z * n_yl + place // (n_grp * n_rep)) * CORES + core
        return (there, (place // n_rep) % n_grp, place % n_rep)

    above, below = device_of((k + 1) % count), device_of((k + count - 1) % count)

    barrier = pltpu.get_barrier_semaphore()

    def greet(device):
        pl.semaphore_signal(barrier, inc=1, device_id=device, device_id_type=MESH)

    greet(above)
    greet(below)

    @pl.loop(1, n_line)
    def _(j):
        greet(on_line((line + j) % n_line))

    @pl.loop(1, n_plane)
    def _(j):
        greet(on_plane((plane + j) % n_plane))

    loads = [
        pltpu.make_async_copy(a, b, load_sem.at[i])
        for i, (a, b) in enumerate(
            ((direction_hbm, direction), (coarse_hbm, coarse), (residual_hbm, residual), (blocks_hbm, blocks))
        )
    ]
    for load in loads:
        load.start()

    back_at = []
    for v in range(faces):
        place = jnp.int32(0)
        for b in range(faces):
            place = jnp.where(facing[0, b] == v, b, place)
        back_at.append(place)

    loads[0].wait()
    for b in range(faces):
        forward_out[b, :block] = direction[facing[0, b]]
    rows8 = lax.broadcasted_iota(jnp.int32, (n_corners, tracks), 0)
    wanted = jnp.zeros((n_corners, tracks), jnp.int32)
    for i in range(n_corners):
        wanted = jnp.where(rows8 == i, back_at[i // per_block] * block + corners[0, i] % block, wanted)
    forward_out[faces - 1, block:] = wanted.astype(jnp.float32)

    loads[1].wait()
    lanes = lax.broadcasted_iota(jnp.int32, (n_corners, LANES), 1)
    half = LANES // CORES
    for zz in range(n_z):
        for q in range(n_yl // CORES):
            first = coarse[:, pl.ds((zz * n_yl + 2 * q) * LANES, LANES)]
            second = coarse[:, pl.ds((zz * n_yl + 2 * q + 1) * LANES, LANES)]
            at = pl.ds(q * LANES, LANES)
            packed[zz * CORES, :, at] = jnp.where(lanes < half, first, pltpu.roll(second, half, 1))
            packed[zz * CORES + 1, :, at] = jnp.where(lanes < half, pltpu.roll(first, half, 1), second)

    pl.semaphore_wait(barrier, n_line + n_plane)

    def remote(source_ref, target_ref, send, recv, device):
        return pltpu.make_async_remote_copy(
            src_ref=source_ref,
            dst_ref=target_ref,
            send_sem=send,
            recv_sem=recv,
            device_id=device,
            device_id_type=MESH,
        )

    forward = []
    for b in range(faces):
        rows = pl.ds(0, block if b < faces - 1 else block + n_corners)
        forward.append(
            remote(forward_out.at[b, rows], forward_in.at[b, rows], forward_send.at[b], forward_recv.at[b], above)
        )
        forward[-1].start()

    def exchange(stage, size, mine, where, source_of, target):
        @pl.loop(1, size)
        def _(j):
            there = (mine + j) % size
            remote(
                source_of(there), target.at[mine], group_send.at[stage], group_recv.at[stage], where(there)
            ).start()

    def all_of(stage, size, target, sems):
        rest = target.at[pl.ds(0, size - 1)]
        return pltpu.make_async_copy(rest, rest, sems.at[stage])

    exchange(0, n_line, line, on_line, lambda there: packed.at[there], columns)
    columns[line] = packed[line]

    rows32 = 32
    zero = (jnp.zeros((rows32, tracks), jnp.float32),) * 2
    loads[2].wait()

    def add_old(i, total):
        r = residual[pl.ds(pl.multiple_of(i * rows32, rows32), rows32)]
        return add_product(total, r, r)

    old = fold(lax.fori_loop(0, faces * block // rows32, add_old, zero))
    for r in range(2 * faces, row_blocks):
        source[r] = jnp.zeros((block, tracks), jnp.float32)
        rounded[0, r] = jnp.zeros((block, tracks), rounded.dtype)
    for b in range(faces):
        source[faces + b] = direction[b]
        rounded[0, faces + b] = direction[b].astype(rounded.dtype)
    loads[3].wait()
    for b in range(faces):
        forward[b].wait_recv()
    for b in range(faces):
        arrived = jnp.where(k > 0, -forward_in[b, :block], 0.0)
        source[b] = arrived
        rounded[0, b] = arrived.astype(rounded.dtype)

    def relaxed(r, now):
        left = jnp.concatenate([blocks[r, j] for j in range(nnz)], axis=1)
        right = jnp.concatenate([rounded[now, pattern[r, j]] for j in range(nnz)], axis=0)
        return source[r] - jnp.dot(left, right, preferred_element_type=jnp.float32)

    for sweep in range(SWEEPS - 1):

        def step(r, carry, now=sweep % 2):
            rounded[1 - now, r] = relaxed(r, now).astype(rounded.dtype)
            return carry

        lax.fori_loop(0, row_blocks, step, 0, unroll=4)
    last = (SWEEPS - 1) % 2

    def step_lower(r, carry):
        back_out[r] = relaxed(r, last)
        return carry

    lax.fori_loop(0, faces, step_lower, 0, unroll=True)

    rows_seg = lax.broadcasted_iota(jnp.int32, (segment, tracks), 0)
    found = jnp.zeros((n_corners, tracks), jnp.float32)
    for i in range(n_corners):
        at = forward_in[faces - 1, block + i : block + i + 1].astype(jnp.int32)
        low = (i % per_block) * segment
        sought = jnp.zeros((8, tracks), jnp.float32)
        for b in range(faces):
            piece = back_out[b, low : low + segment]
            hit = jnp.where(rows_seg + (b * block + low) == at, piece, 0.0)
            sought = sought + jnp.sum(hit.reshape(segment // 8, 8, tracks), axis=0)
        found = jnp.where(rows8 == i, jnp.sum(sought, axis=0, keepdims=True), found)
    corner_out[...] = found
    corner_copy = remote(corner_out, corner_in, corner_send, corner_recv, below)
    corner_copy.start()
    back = [
        remote(back_out.at[b], back_in.at[b], back_send.at[b], back_recv.at[b], below) for b in range(faces)
    ]
    for copy in back:
        copy.start()

    def step_upper(r, carry):
        upper[pl.ds(pl.multiple_of((r - faces) * block, block), block)] = relaxed(r, last)
        return carry

    lax.fori_loop(faces, 2 * faces, step_upper, 0, unroll=True)
    own = jnp.zeros((n_corners, tracks), jnp.float32)
    for i in range(n_corners):
        own = jnp.where(rows8 == i, upper[pl.ds(corners[0, i], 1)], own)

    all_of(0, n_line, columns, group_recv).wait()
    turned[...] = columns[...].reshape(n_line * n_corners, n_plane * n_corners).T

    corner_copy.wait_recv()
    at_corners = jnp.where(k < count - 1, corner_in[...], 0.0)
    totals[line] = own + at_corners
    exchange(1, n_line, line, on_line, lambda there: totals.at[line], totals)
    own_jump = own - at_corners
    own_residual = jnp.zeros((n_corners, tracks), jnp.float32)
    for i in range(n_corners):
        own_residual = jnp.where(rows8 == i, residual[pl.ds(corners[0, i], 1)], own_residual)

    all_of(1, n_line, totals, group_recv).wait()
    part[...] = jnp.dot(
        turned[...],
        totals[...].reshape(n_line * n_corners, tracks),
        precision=lax.Precision.HIGHEST,
        preferred_element_type=jnp.float32,
    ).reshape(n_plane, n_corners, tracks)
    exchange(2, n_plane, plane, on_plane, lambda there: part.at[there], part_in)
    part_in[plane] = part[plane]

    for copy in back:
        copy.wait_recv()
    rows_in = lax.broadcasted_iota(jnp.int32, (rows32, tracks), 0)
    cross, curve = zero, zero
    for i in range(n_corners):
        for piece in range(segment // rows32):
            start = i * segment + piece * rows32
            v, low = start // block, start % block
            mapped = jnp.where(k < count - 1, back_in[back_at[v], low : low + rows32], 0.0)
            jump = upper[start : start + rows32] - mapped
            image[start : start + rows32] = jump
            jump = jnp.where(rows_in + start == corners[0, i], 0.0, jump)
            cross = add_product(cross, residual[start : start + rows32], jump)
            curve = add_product(curve, jump, jump)
    cross = fold((cross[0].reshape(4, 8, tracks), cross[1].reshape(4, 8, tracks)))
    curve = fold((curve[0].reshape(4, 8, tracks), curve[1].reshape(4, 8, tracks)))

    all_of(2, n_plane, part_in, group_recv).wait()
    coarse_part = jnp.sum(part_in[...], axis=0)
    at_nodes = own_jump + coarse_part
    cross = fold(tuple(v.reshape(n_corners, tracks) for v in add_product(cross, own_residual, at_nodes)))
    curve = fold(tuple(v.reshape(n_corners, tracks) for v in add_product(curve, at_nodes, at_nodes)))

    mine = jnp.concatenate([old[0], cross[0], curve[0], old[1], cross[1], curve[1]], axis=1)
    sums_plane[plane] = mine
    exchange(3, n_plane, plane, on_plane, lambda there: sums_plane.at[plane], sums_plane)
    for i in range(n_corners):
        for piece in range(segment // rows32):
            start = i * segment + piece * rows32
            added = jnp.where(rows_in + start == corners[0, i], coarse_part[i : i + 1], 0.0)
            image[start : start + rows32] = image[start : start + rows32] + added

    def total_of(buffer):
        pair = fold((buffer[:, :, : 3 * tracks], buffer[:, :, 3 * tracks :]))
        return tuple(v.reshape(1, 3 * tracks) for v in tidy(pair))

    all_of(3, n_plane, sums_plane, group_recv).wait()
    sums_line[line] = jnp.concatenate(total_of(sums_plane), axis=1)
    exchange(4, n_line, line, on_line, lambda there: sums_line.at[line], sums_line)
    all_of(4, n_line, sums_line, group_recv).wait()
    pair = total_of(sums_line)
    old, cross, curve = (
        tuple(v[:, i * tracks : (i + 1) * tracks] for v in pair) for i in range(3)
    )
    length = cross[0] / curve[0]
    scale = 2.0**-14
    old, cross, curve = (tuple(v * scale for v in pair) for pair in (old, cross, curve))
    inner, inner_low = two_product(-length, curve[0])
    inner = tidy(pair_add((2.0 * cross[0], 2.0 * cross[1]), (inner, inner_low - length * curve[1])))
    outer, outer_low = two_product(-length, inner[0])
    new = tidy(pair_add(old, (outer, outer_low - length * inner[1])))
    factors[0:1] = length
    factors[1:2] = jnp.maximum(new[0], 0.0) / old[0]

    for copy in forward + back:
        copy.wait_send()
    corner_copy.wait_send()
    for stage, (size, buffer) in enumerate(
        ((n_line, columns), (n_line, totals), (n_plane, part_in), (n_plane, sums_plane), (n_line, sums_line))
    ):
        all_of(stage, size, buffer, group_send).wait()


def per_device(sizes, residual, direction, sub_blocks, pattern, facing, corners, coarse_inverse):
    n_z, n_yl, n_grp, n_rep = sizes
    n_line, n_plane = n_z * CORES, n_yl * n_grp * n_rep
    face_rows, tracks = residual.shape
    row_blocks, nnz, block, _ = sub_blocks.shape
    faces, n_corners = facing.shape[1], corners.shape[1]
    f32, vmem = jnp.float32, pltpu.VMEM
    dma = pltpu.SemaphoreType.DMA
    image, factors = pl.pallas_call(
        functools.partial(kernel, sizes),
        out_shape=(jax.ShapeDtypeStruct((face_rows, tracks), f32), jax.ShapeDtypeStruct((2, tracks), f32)),
        in_specs=[pl.BlockSpec(memory_space=pltpu.SMEM)] * 3 + [pl.BlockSpec(memory_space=pl.ANY)] * 4,
        out_specs=(pl.BlockSpec(memory_space=vmem),) * 2,
        scratch_shapes=[
            vmem((face_rows, tracks), f32),
            vmem((faces, block, tracks), f32),
            vmem(sub_blocks.shape, sub_blocks.dtype),
            vmem(coarse_inverse.shape, f32),
            vmem((row_blocks, block, tracks), f32),
            vmem((2, row_blocks, block, tracks), jnp.bfloat16),
            vmem((face_rows, tracks), f32),
            vmem((faces, block + n_corners, tracks), f32),
            vmem((faces, block + n_corners, tracks), f32),
            vmem((faces, block, tracks), f32),
            vmem((faces, block, tracks), f32),
            vmem((n_corners, tracks), f32),
            vmem((n_corners, tracks), f32),
            vmem((n_line, n_corners, n_plane * n_corners), f32),
            vmem((n_line, n_corners, n_plane * n_corners), f32),
            vmem((n_plane * n_corners, n_line * n_corners), f32),
            vmem((n_line, n_corners, tracks), f32),
            vmem((n_plane, n_corners, tracks), f32),
            vmem((n_plane, n_corners, tracks), f32),
            vmem((n_plane, 1, 6 * tracks), f32),
            vmem((n_line, 1, 6 * tracks), f32),
            dma((4,)),
            dma((faces,)),
            dma((faces,)),
            dma((faces,)),
            dma((faces,)),
            dma,
            dma,
            dma((5,)),
            dma((5,)),
        ],
        compiler_params=pltpu.CompilerParams(
            collective_id=0, has_side_effects=True, vmem_limit_bytes=32 * 1024 * 1024
        ),
    )(
        pattern,
        facing,
        corners,
        residual,
        direction.reshape(faces, block, tracks),
        sub_blocks,
        coarse_inverse,
    )
    residual_new = residual - factors[0:1] * image
    return residual_new, residual_new + factors[1:2] * direction


def solution(mesh):
    n_sub, n_grp, n_rep = (mesh.shape[a] for a in AXES)
    n_yl = 4 if n_sub % (4 * CORES) == 0 else 2
    sizes = (n_sub // (n_yl * CORES), n_yl, n_grp, n_rep)
    rows = P(AXES, None)
    return jax.shard_map(
        functools.partial(per_device, sizes),
        mesh=mesh,
        in_specs=(rows, rows, P(AXES, None, None, None), rows, rows, rows, rows),
        out_specs=(rows, rows),
        check_vma=False,
    )
```

```python
import functools

import jax
import jax.numpy as jnp
from jax import lax
from jax.experimental import pallas as pl
from jax.experimental.pallas import tpu as pltpu
from jax.sharding import PartitionSpec as P

MESH = pl.DeviceIdType.MESH
AXES = ("sub", "grp", "rep")
SWEEPS = 3
CORES = 2
LANES = 128


def two_sum(a, b):
    s = a + b
    t = s - a
    return s, (a - (s - t)) + (b - t)


def split(a):
    c = a * 4097.0
    hi = c - (c - a)
    return hi, a - hi


def two_product(a, b):
    p = a * b
    ah, al = split(a)
    bh, bl = split(b)
    return p, ((ah * bh - p) + ah * bl + al * bh) + al * bl


def pair_add(a, b):
    s, e = two_sum(a[0], b[0])
    return s, e + (a[1] + b[1])


def tidy(a):
    s = a[0] + a[1]
    return s, a[1] - (s - a[0])


def add_product(total, a, b):
    p, e = two_product(a, b)
    return pair_add(total, (p, e))


def fold(pair, axis=0):
    while pair[0].shape[axis] > 1:
        half = pair[0].shape[axis] // 2
        pair = pair_add(
            tuple(lax.slice_in_dim(v, 0, half, axis=axis) for v in pair),
            tuple(lax.slice_in_dim(v, half, 2 * half, axis=axis) for v in pair),
        )
    return pair


def kernel(
    sizes,
    pattern_hbm,
    facing_hbm,
    corners_hbm,
    residual_hbm,
    direction_hbm,
    blocks_hbm,
    coarse_hbm,
    image,
    factors,
    pattern,
    facing,
    corners,
    residual,
    direction,
    blocks,
    coarse,
    source,
    rounded,
    upper,
    forward_out,
    forward_in,
    back_out,
    back_in,
    corner_out,
    corner_in,
    packed,
    columns,
    turned,
    totals,
    part,
    part_in,
    sums_plane,
    sums_line,
    sums_pair,
    load_sem,
    forward_send,
    forward_recv,
    back_send,
    back_recv,
    corner_send,
    corner_recv,
    group_send,
    group_recv,
    pair_send,
    pair_recv,
):
    n_z, n_yl, n_grp, n_rep = sizes
    n_line, n_plane = n_z * CORES, n_yl * n_grp * n_rep
    count = n_line * n_plane
    faces, block, tracks = forward_in.shape[0], direction.shape[1], direction.shape[2]
    row_blocks, nnz = blocks.shape[:2]
    n_corners = corners.shape[1]
    segment = faces * block // n_corners
    per_block = block // segment

    sub, grp, rep = (lax.axis_index(a) for a in AXES)
    k = (sub * n_grp + grp) * n_rep + rep
    core, yl, z = sub % CORES, (sub // CORES) % n_yl, sub // (CORES * n_yl)
    line = core * n_z + z
    plane = (yl * n_grp + grp) * n_rep + rep

    def device_of(index):
        return (index // (n_grp * n_rep), (index // n_rep) % n_grp, index % n_rep)

    def ring(step, size):
        return min(step, size - step)

    z_steps = sorted(range(1, n_z), key=lambda step: -ring(step, n_z))

    def plane_hops(step):
        over_y = ring(step // (n_grp * n_rep), n_yl)
        if step % n_rep:
            over_y = n_yl - over_y
        return over_y + ring(step // n_rep % n_grp, n_grp)

    plane_steps = sorted(range(1, n_plane), key=lambda step: -plane_hops(step))

    def plane_at(step):
        there_yl = (yl + step // (n_grp * n_rep)) % n_yl
        there_grp = (grp + step // n_rep % n_grp) % n_grp
        return (there_yl * n_grp + there_grp) * n_rep + (rep + step) % n_rep

    def on_line(place):
        return ((place % n_z * n_yl + yl) * CORES + place // n_z, grp, rep)

    def on_plane(place):
        there = (z * n_yl + place // (n_grp * n_rep)) * CORES + core
        return (there, (place // n_rep) % n_grp, place % n_rep)

    def along_z(place):
        return ((place * n_yl + yl) * CORES + core, grp, rep)

    sibling = ((z * n_yl + yl) * CORES + 1 - core, grp, rep)
    above, below = device_of((k + 1) % count), device_of((k + count - 1) % count)

    barrier = pltpu.get_barrier_semaphore()

    def greet(device):
        pl.semaphore_signal(barrier, inc=1, device_id=device, device_id_type=MESH)

    greet(above)
    greet(below)
    for step in z_steps:
        for other in range(CORES):
            greet((((z + step) % n_z * n_yl + yl) * CORES + other, grp, rep))
    for step in plane_steps:
        greet(on_plane(plane_at(step)))
    greet(sibling)

    loads = [
        pltpu.make_async_copy(a, b, load_sem.at[i])
        for i, (a, b) in enumerate(
            (
                (facing_hbm, facing),
                (corners_hbm, corners),
                (direction_hbm, direction),
                (coarse_hbm, coarse),
                (residual_hbm, residual),
                (pattern_hbm, pattern),
                (blocks_hbm, blocks),
            )
        )
    ]
    for load in loads:
        load.start()
    for load in loads[:3]:
        load.wait()

    back_at = []
    for v in range(faces):
        place = jnp.int32(0)
        for b in range(faces):
            place = jnp.where(facing[0, b] == v, b, place)
        back_at.append(place)

    for b in range(faces):
        forward_out[b, :block] = direction[facing[0, b]]
    rows8 = lax.broadcasted_iota(jnp.int32, (n_corners, tracks), 0)
    wanted = jnp.zeros((n_corners, tracks), jnp.int32)
    for i in range(n_corners):
        wanted = jnp.where(rows8 == i, back_at[i // per_block] * block + corners[0, i] % block, wanted)
    forward_out[faces - 1, block:] = wanted.astype(jnp.float32)

    loads[3].wait()
    lanes = lax.broadcasted_iota(jnp.int32, (n_corners, LANES), 1)
    half = LANES // CORES
    for zz in range(n_z):
        for q in range(n_yl // CORES):
            first = coarse[:, pl.ds((zz * n_yl + 2 * q) * LANES, LANES)]
            second = coarse[:, pl.ds((zz * n_yl + 2 * q + 1) * LANES, LANES)]
            at = pl.ds(q * LANES, LANES)
            packed[zz, :, at] = jnp.where(lanes < half, first, pltpu.roll(second, half, 1))
            packed[n_z + zz, :, at] = jnp.where(lanes < half, pltpu.roll(first, half, 1), second)

    pl.semaphore_wait(barrier, n_line + n_plane)

    def remote(source_ref, target_ref, send, recv, device):
        return pltpu.make_async_remote_copy(
            src_ref=source_ref,
            dst_ref=target_ref,
            send_sem=send,
            recv_sem=recv,
            device_id=device,
            device_id_type=MESH,
        )

    forward = []
    for b in range(faces):
        rows = pl.ds(0, block if b < faces - 1 else block + n_corners)
        forward.append(
            remote(forward_out.at[b, rows], forward_in.at[b, rows], forward_send.at[b], forward_recv.at[b], above)
        )
        forward[-1].start()

    def exchange(stage, size, mine, where, source_of, target):
        @pl.loop(1, size)
        def _(j):
            there = (mine + j) % size
            remote(
                source_of(there), target.at[mine], group_send.at[stage], group_recv.at[stage], where(there)
            ).start()

    def send_all(stage, places, where, mine, source_of, target):
        for there in places:
            remote(
                source_of(there), target.at[mine], group_send.at[stage], group_recv.at[stage], where(there)
            ).start()

    def over_z(stage, source_of, target):
        send_all(stage, [(z + step) % n_z for step in z_steps], along_z, z, source_of, target)

    def over_plane(stage, source_of, target):
        send_all(stage, [plane_at(step) for step in plane_steps], on_plane, plane, source_of, target)

    def all_of(stage, size, target, sems):
        rest = target.at[pl.ds(0, size - 1)]
        return pltpu.make_async_copy(rest, rest, sems.at[stage])

    exchange(0, n_line, line, on_line, lambda there: packed.at[there], columns)
    columns[line] = packed[line]

    rows32 = 32
    zero = (jnp.zeros((rows32, tracks), jnp.float32),) * 2
    loads[4].wait()

    def add_old(i, total):
        r = residual[pl.ds(pl.multiple_of(i * rows32, rows32), rows32)]
        return add_product(total, r, r)

    old = fold(lax.fori_loop(0, faces * block // rows32, add_old, zero))
    for r in range(2 * faces, row_blocks):
        source[r] = jnp.zeros((block, tracks), jnp.float32)
        rounded[0, r] = jnp.zeros((block, tracks), rounded.dtype)
    for b in range(faces):
        source[faces + b] = direction[b]
        rounded[0, faces + b] = direction[b].astype(rounded.dtype)
    loads[5].wait()
    loads[6].wait()
    for b in range(faces):
        forward[b].wait_recv()
    for b in range(faces):
        arrived = jnp.where(k > 0, -forward_in[b, :block], 0.0)
        source[b] = arrived
        rounded[0, b] = arrived.astype(rounded.dtype)

    def relaxed(pair, now):
        rows = (2 * pair, 2 * pair + 1)
        left = [jnp.concatenate([blocks[r, j] for j in range(nnz)], axis=1) for r in rows]
        right = [jnp.concatenate([rounded[now, pattern[j, r]] for j in range(nnz)], axis=0) for r in rows]
        product = jnp.dot(
            jnp.concatenate(left, axis=0), jnp.concatenate(right, axis=1), preferred_element_type=jnp.float32
        )
        return source[rows[0]] - product[:block, :tracks], source[rows[1]] - product[block:, tracks:]

    for sweep in range(SWEEPS - 1):

        def step(pair, carry, now=sweep % 2):
            first, second = relaxed(pair, now)
            rounded[1 - now, 2 * pair] = first.astype(rounded.dtype)
            rounded[1 - now, 2 * pair + 1] = second.astype(rounded.dtype)
            return carry

        lax.fori_loop(0, row_blocks // 2, step, 0, unroll=2)
    last = (SWEEPS - 1) % 2
    for pair in range(faces // 2):
        back_out[2 * pair], back_out[2 * pair + 1] = relaxed(pair, last)

    rows_seg = lax.broadcasted_iota(jnp.int32, (segment, tracks), 0)
    found = jnp.zeros((n_corners, tracks), jnp.float32)
    for i in range(n_corners):
        at = forward_in[faces - 1, block + i : block + i + 1].astype(jnp.int32)
        low = (i % per_block) * segment
        sought = jnp.zeros((8, tracks), jnp.float32)
        for b in range(faces):
            piece = back_out[b, low : low + segment]
            hit = jnp.where(rows_seg + (b * block + low) == at, piece, 0.0)
            sought = sought + jnp.sum(hit.reshape(segment // 8, 8, tracks), axis=0)
        found = jnp.where(rows8 == i, jnp.sum(sought, axis=0, keepdims=True), found)
    corner_out[...] = found
    corner_copy = remote(corner_out, corner_in, corner_send, corner_recv, below)
    corner_copy.start()
    back = [
        remote(back_out.at[b], back_in.at[b], back_send.at[b], back_recv.at[b], below) for b in range(faces)
    ]
    for copy in back:
        copy.start()

    for pair in range(faces // 2):
        start = 2 * pair * block
        upper[start : start + block], upper[start + block : start + 2 * block] = relaxed(faces // 2 + pair, last)
    own = jnp.zeros((n_corners, tracks), jnp.float32)
    for i in range(n_corners):
        own = jnp.where(rows8 == i, upper[pl.ds(corners[0, i], 1)], own)

    all_of(0, n_line, columns, group_recv).wait()
    turned[...] = columns[...].reshape(n_line * n_corners, n_plane * n_corners).T

    corner_copy.wait_recv()
    at_corners = jnp.where(k < count - 1, corner_in[...], 0.0)
    totals[core, z] = own + at_corners
    over_z(1, lambda there: totals.at[core, z], totals.at[core])
    own_jump = own - at_corners
    own_residual = jnp.zeros((n_corners, tracks), jnp.float32)
    for i in range(n_corners):
        own_residual = jnp.where(rows8 == i, residual[pl.ds(corners[0, i], 1)], own_residual)

    all_of(1, n_z, totals.at[core], group_recv).wait()
    to_sibling = remote(totals.at[core], totals.at[core], pair_send.at[0], pair_recv.at[0], sibling)
    to_sibling.start()
    to_sibling.wait_recv()
    part[...] = jnp.dot(
        turned[...],
        totals[...].reshape(n_line * n_corners, tracks),
        precision=lax.Precision.HIGHEST,
        preferred_element_type=jnp.float32,
    ).reshape(n_plane, n_corners, tracks)
    over_plane(2, lambda there: part.at[there], part_in)
    part_in[plane] = part[plane]

    for copy in back:
        copy.wait_recv()
    rows_in = lax.broadcasted_iota(jnp.int32, (rows32, tracks), 0)
    cross, curve = zero, zero
    for i in range(n_corners):
        for piece in range(segment // rows32):
            start = i * segment + piece * rows32
            v, low = start // block, start % block
            mapped = jnp.where(k < count - 1, back_in[back_at[v], low : low + rows32], 0.0)
            jump = upper[start : start + rows32] - mapped
            image[start : start + rows32] = jump
            jump = jnp.where(rows_in + start == corners[0, i], 0.0, jump)
            cross = add_product(cross, residual[start : start + rows32], jump)
            curve = add_product(curve, jump, jump)
    cross = fold((cross[0].reshape(4, 8, tracks), cross[1].reshape(4, 8, tracks)))
    curve = fold((curve[0].reshape(4, 8, tracks), curve[1].reshape(4, 8, tracks)))

    all_of(2, n_plane, part_in, group_recv).wait()
    coarse_part = jnp.sum(part_in[...], axis=0)
    at_nodes = own_jump + coarse_part
    cross = fold(tuple(v.reshape(n_corners, tracks) for v in add_product(cross, own_residual, at_nodes)))
    curve = fold(tuple(v.reshape(n_corners, tracks) for v in add_product(curve, at_nodes, at_nodes)))

    mine = jnp.concatenate([old[0], cross[0], curve[0], old[1], cross[1], curve[1]], axis=1)
    sums_plane[plane] = mine
    over_plane(3, lambda there: sums_plane.at[plane], sums_plane)
    for i in range(n_corners):
        for piece in range(segment // rows32):
            start = i * segment + piece * rows32
            added = jnp.where(rows_in + start == corners[0, i], coarse_part[i : i + 1], 0.0)
            image[start : start + rows32] = image[start : start + rows32] + added

    def total_of(buffer):
        pair = fold((buffer[:, :, : 3 * tracks], buffer[:, :, 3 * tracks :]))
        return tuple(v.reshape(1, 3 * tracks) for v in tidy(pair))

    all_of(3, n_plane, sums_plane, group_recv).wait()
    sums_line[z] = jnp.concatenate(total_of(sums_plane), axis=1)
    over_z(4, lambda there: sums_line.at[z], sums_line)
    all_of(4, n_z, sums_line, group_recv).wait()
    sums_pair[core] = jnp.concatenate(total_of(sums_line), axis=1)
    sums_to_sibling = remote(sums_pair.at[core], sums_pair.at[core], pair_send.at[1], pair_recv.at[1], sibling)
    sums_to_sibling.start()
    sums_to_sibling.wait_recv()
    pair = total_of(sums_pair)
    old, cross, curve = (
        tuple(v[:, i * tracks : (i + 1) * tracks] for v in pair) for i in range(3)
    )
    length = cross[0] / curve[0]
    scale = 2.0**-14
    old, cross, curve = (tuple(v * scale for v in pair) for pair in (old, cross, curve))
    inner, inner_low = two_product(-length, curve[0])
    inner = tidy(pair_add((2.0 * cross[0], 2.0 * cross[1]), (inner, inner_low - length * curve[1])))
    outer, outer_low = two_product(-length, inner[0])
    new = tidy(pair_add(old, (outer, outer_low - length * inner[1])))
    factors[0:1] = length
    factors[1:2] = jnp.maximum(new[0], 0.0) / old[0]

    for copy in forward + back + [corner_copy, to_sibling, sums_to_sibling]:
        copy.wait_send()
    for stage, (size, buffer) in enumerate(
        ((n_line, columns), (n_z, totals.at[0]), (n_plane, part_in), (n_plane, sums_plane), (n_z, sums_line))
    ):
        all_of(stage, size, buffer, group_send).wait()


def per_device(sizes, residual, direction, sub_blocks, pattern, facing, corners, coarse_inverse):
    n_z, n_yl, n_grp, n_rep = sizes
    n_line, n_plane = n_z * CORES, n_yl * n_grp * n_rep
    face_rows, tracks = residual.shape
    row_blocks, nnz, block, _ = sub_blocks.shape
    faces, n_corners = facing.shape[1], corners.shape[1]
    f32, vmem, smem = jnp.float32, pltpu.VMEM, pltpu.SMEM
    dma = pltpu.SemaphoreType.DMA
    image, factors = pl.pallas_call(
        functools.partial(kernel, sizes),
        out_shape=(jax.ShapeDtypeStruct((face_rows, tracks), f32), jax.ShapeDtypeStruct((2, tracks), f32)),
        in_specs=[pl.BlockSpec(memory_space=pltpu.HBM)] * 7,
        out_specs=(pl.BlockSpec(memory_space=vmem),) * 2,
        scratch_shapes=[
            smem((nnz, row_blocks), jnp.int32),
            smem(facing.shape, jnp.int32),
            smem(corners.shape, jnp.int32),
            vmem((face_rows, tracks), f32),
            vmem((faces, block, tracks), f32),
            vmem(sub_blocks.shape, sub_blocks.dtype),
            vmem(coarse_inverse.shape, f32),
            vmem((row_blocks, block, tracks), f32),
            vmem((2, row_blocks, block, tracks), jnp.bfloat16),
            vmem((face_rows, tracks), f32),
            vmem((faces, block + n_corners, tracks), f32),
            vmem((faces, block + n_corners, tracks), f32),
            vmem((faces, block, tracks), f32),
            vmem((faces, block, tracks), f32),
            vmem((n_corners, tracks), f32),
            vmem((n_corners, tracks), f32),
            vmem((n_line, n_corners, n_plane * n_corners), f32),
            vmem((n_line, n_corners, n_plane * n_corners), f32),
            vmem((n_plane * n_corners, n_line * n_corners), f32),
            vmem((CORES, n_z, n_corners, tracks), f32),
            vmem((n_plane, n_corners, tracks), f32),
            vmem((n_plane, n_corners, tracks), f32),
            vmem((n_plane, 1, 6 * tracks), f32),
            vmem((n_z, 1, 6 * tracks), f32),
            vmem((CORES, 1, 6 * tracks), f32),
            dma((7,)),
            dma((faces,)),
            dma((faces,)),
            dma((faces,)),
            dma((faces,)),
            dma,
            dma,
            dma((5,)),
            dma((5,)),
            dma((2,)),
            dma((2,)),
        ],
        compiler_params=pltpu.CompilerParams(
            collective_id=0, has_side_effects=True, vmem_limit_bytes=62 * 1024 * 1024
        ),
    )(
        pattern.T,
        facing,
        corners,
        residual,
        direction.reshape(faces, block, tracks),
        sub_blocks,
        coarse_inverse,
    )
    residual_new = residual - factors[0:1] * image
    return residual_new, residual_new + factors[1:2] * direction


def solution(mesh):
    n_sub, n_grp, n_rep = (mesh.shape[a] for a in AXES)
    n_yl = 4 if n_sub % (4 * CORES) == 0 else 2
    sizes = (n_sub // (n_yl * CORES), n_yl, n_grp, n_rep)
    rows = P(AXES, None)
    return jax.shard_map(
        functools.partial(per_device, sizes),
        mesh=mesh,
        in_specs=(rows, rows, P(AXES, None, None, None), rows, rows, rows, rows),
        out_specs=(rows, rows),
        check_vma=False,
    )
```

```python
import functools

import jax
import jax.numpy as jnp
from jax import lax
from jax.experimental import pallas as pl
from jax.experimental.pallas import tpu as pltpu
from jax.sharding import PartitionSpec as P

MESH = pl.DeviceIdType.MESH
AXES = ("sub", "grp", "rep")
SWEEPS = 3
CORES = 2
LANES = 128


def two_sum(a, b):
    s = a + b
    t = s - a
    return s, (a - (s - t)) + (b - t)


def split(a):
    c = a * 4097.0
    hi = c - (c - a)
    return hi, a - hi


def two_product(a, b):
    p = a * b
    ah, al = split(a)
    bh, bl = split(b)
    return p, ((ah * bh - p) + ah * bl + al * bh) + al * bl


def pair_add(a, b):
    s, e = two_sum(a[0], b[0])
    return s, e + (a[1] + b[1])


def tidy(a):
    s = a[0] + a[1]
    return s, a[1] - (s - a[0])


def add_product(total, a, b):
    p, e = two_product(a, b)
    return pair_add(total, (p, e))


def fold(pair, axis=0):
    while pair[0].shape[axis] > 1:
        half = pair[0].shape[axis] // 2
        pair = pair_add(
            tuple(lax.slice_in_dim(v, 0, half, axis=axis) for v in pair),
            tuple(lax.slice_in_dim(v, half, 2 * half, axis=axis) for v in pair),
        )
    return pair


def kernel(
    sizes,
    pattern_hbm,
    facing_hbm,
    corners_hbm,
    residual_hbm,
    direction_hbm,
    blocks_hbm,
    coarse_hbm,
    image_hbm,
    factors,
    pattern,
    facing,
    corners,
    image,
    residual,
    direction,
    blocks,
    coarse,
    source,
    rounded,
    rounded_next,
    upper,
    forward_out,
    forward_in,
    back_out,
    back_in,
    corner_out,
    corner_in,
    packed,
    columns,
    turned,
    totals,
    part,
    part_in,
    sums_plane,
    sums_line,
    sums_pair,
    load_sem,
    forward_send,
    forward_recv,
    back_send,
    back_recv,
    corner_send,
    corner_recv,
    group_send,
    group_recv,
    pair_send,
    pair_recv,
):
    n_z, n_yl, n_grp, n_rep = sizes
    n_line, n_plane = n_z * CORES, n_yl * n_grp * n_rep
    count = n_line * n_plane
    faces, block, tracks = forward_in.shape[0], direction.shape[1], direction.shape[2]
    row_blocks, nnz = blocks.shape[:2]
    n_corners = corners.shape[1]
    segment = faces * block // n_corners
    per_block = block // segment

    sub, grp, rep = (lax.axis_index(a) for a in AXES)
    k = (sub * n_grp + grp) * n_rep + rep
    core, yl, z = sub % CORES, (sub // CORES) % n_yl, sub // (CORES * n_yl)
    line = core * n_z + z
    plane = (yl * n_grp + grp) * n_rep + rep

    def device_of(index):
        return (index // (n_grp * n_rep), (index // n_rep) % n_grp, index % n_rep)

    def ring(step, size):
        return min(step, size - step)

    z_steps = sorted(range(1, n_z), key=lambda step: -ring(step, n_z))

    def plane_hops(step):
        over_y = ring(step // (n_grp * n_rep), n_yl)
        if step % n_rep:
            over_y = n_yl - over_y
        return over_y + ring(step // n_rep % n_grp, n_grp)

    plane_steps = sorted(range(1, n_plane), key=lambda step: -plane_hops(step))

    def plane_at(step):
        there_yl = (yl + step // (n_grp * n_rep)) % n_yl
        there_grp = (grp + step // n_rep % n_grp) % n_grp
        return (there_yl * n_grp + there_grp) * n_rep + (rep + step) % n_rep

    def on_line(place):
        return ((place % n_z * n_yl + yl) * CORES + place // n_z, grp, rep)

    def on_plane(place):
        there = (z * n_yl + place // (n_grp * n_rep)) * CORES + core
        return (there, (place // n_rep) % n_grp, place % n_rep)

    def along_z(place):
        return ((place * n_yl + yl) * CORES + core, grp, rep)

    sibling = ((z * n_yl + yl) * CORES + 1 - core, grp, rep)
    above, below = device_of((k + 1) % count), device_of((k + count - 1) % count)

    barrier = pltpu.get_barrier_semaphore()

    def greet(device):
        pl.semaphore_signal(barrier, inc=1, device_id=device, device_id_type=MESH)

    greet(above)
    greet(below)
    for step in z_steps:
        for other in range(CORES):
            greet((((z + step) % n_z * n_yl + yl) * CORES + other, grp, rep))
    for step in plane_steps:
        greet(on_plane(plane_at(step)))
    greet(sibling)

    loads = [
        pltpu.make_async_copy(a, b, load_sem.at[i])
        for i, (a, b) in enumerate(
            (
                (facing_hbm, facing),
                (corners_hbm, corners),
                (direction_hbm, direction),
                (coarse_hbm, coarse),
                (residual_hbm, residual),
                (pattern_hbm, pattern),
                (blocks_hbm, blocks),
            )
        )
    ]
    for load in loads:
        load.start()
    for load in loads[:3]:
        load.wait()

    back_at = []
    for v in range(faces):
        place = jnp.int32(0)
        for b in range(faces):
            place = jnp.where(facing[0, b] == v, b, place)
        back_at.append(place)

    for b in range(faces):
        forward_out[b, :block] = direction[facing[0, b]]
    rows8 = lax.broadcasted_iota(jnp.int32, (n_corners, tracks), 0)
    wanted = jnp.zeros((n_corners, tracks), jnp.int32)
    for i in range(n_corners):
        wanted = jnp.where(rows8 == i, back_at[i // per_block] * block + corners[0, i] % block, wanted)
    forward_out[faces - 1, block:] = wanted.astype(jnp.float32)

    loads[3].wait()
    lanes = lax.broadcasted_iota(jnp.int32, (n_corners, LANES), 1)
    half = LANES // CORES
    for zz in range(n_z):
        for q in range(n_yl // CORES):
            first = coarse[:, pl.ds((zz * n_yl + 2 * q) * LANES, LANES)]
            second = coarse[:, pl.ds((zz * n_yl + 2 * q + 1) * LANES, LANES)]
            at = pl.ds(q * LANES, LANES)
            packed[zz, :, at] = jnp.where(lanes < half, first, pltpu.roll(second, half, 1))
            packed[n_z + zz, :, at] = jnp.where(lanes < half, pltpu.roll(first, half, 1), second)

    pl.semaphore_wait(barrier, n_line + n_plane)

    def remote(source_ref, target_ref, send, recv, device):
        return pltpu.make_async_remote_copy(
            src_ref=source_ref,
            dst_ref=target_ref,
            send_sem=send,
            recv_sem=recv,
            device_id=device,
            device_id_type=MESH,
        )

    forward = []
    for b in range(faces):
        rows = pl.ds(0, block if b < faces - 1 else block + n_corners)
        forward.append(
            remote(forward_out.at[b, rows], forward_in.at[b, rows], forward_send.at[b], forward_recv.at[b], above)
        )
        forward[-1].start()

    def exchange(stage, size, mine, where, source_of, target):
        @pl.loop(1, size)
        def _(j):
            there = (mine + j) % size
            remote(
                source_of(there), target.at[mine], group_send.at[stage], group_recv.at[stage], where(there)
            ).start()

    def send_all(stage, places, where, mine, source_of, target):
        for there in places:
            remote(
                source_of(there), target.at[mine], group_send.at[stage], group_recv.at[stage], where(there)
            ).start()

    def over_z(stage, source_of, target):
        send_all(stage, [(z + step) % n_z for step in z_steps], along_z, z, source_of, target)

    def over_plane(stage, source_of, target):
        send_all(stage, [plane_at(step) for step in plane_steps], on_plane, plane, source_of, target)

    def all_of(stage, size, target, sems):
        rest = target.at[pl.ds(0, size - 1)]
        return pltpu.make_async_copy(rest, rest, sems.at[stage])

    exchange(0, n_line, line, on_line, lambda there: packed.at[there], columns)
    columns[line] = packed[line]

    rows32 = 32
    zero = (jnp.zeros((rows32, tracks), jnp.float32),) * 2
    loads[4].wait()

    def add_old(i, total):
        r = residual[pl.ds(pl.multiple_of(i * rows32, rows32), rows32)]
        return add_product(total, r, r)

    old = fold(lax.fori_loop(0, faces * block // rows32, add_old, zero))
    for r in range(2 * faces, row_blocks):
        source[r] = jnp.zeros((block, tracks), jnp.float32)
        rounded[r] = jnp.zeros((block, tracks), rounded.dtype)
    for b in range(faces):
        source[faces + b] = direction[b]
        rounded[faces + b] = direction[b].astype(rounded.dtype)
    loads[5].wait()
    loads[6].wait()
    for b in range(faces):
        forward[b].wait_recv()
        arrived = jnp.where(k > 0, -forward_in[b, :block], 0.0)
        source[b] = arrived
        rounded[b] = arrived.astype(rounded.dtype)

    def relaxed(r, now):
        left = jnp.concatenate([blocks[r, j] for j in range(nnz)], axis=1)
        right = jnp.concatenate([now[pattern[j, r]] for j in range(nnz)], axis=0)
        return source[r] - jnp.dot(left, right, preferred_element_type=jnp.float32)

    now, later = rounded, rounded_next
    for _ in range(SWEEPS - 1):

        def step(r, carry, now=now, later=later):
            later[r] = relaxed(r, now).astype(later.dtype)
            return carry

        lax.fori_loop(0, row_blocks, step, 0, unroll=True)
        now, later = later, now

    def step_lower(r, carry, now=now):
        back_out[r] = relaxed(r, now)
        return carry

    lax.fori_loop(0, faces, step_lower, 0, unroll=True)

    rows_seg = lax.broadcasted_iota(jnp.int32, (segment, tracks), 0)
    found = jnp.zeros((n_corners, tracks), jnp.float32)
    for i in range(n_corners):
        at = forward_in[faces - 1, block + i : block + i + 1].astype(jnp.int32)
        low = (i % per_block) * segment
        sought = jnp.zeros((8, tracks), jnp.float32)
        for b in range(faces):
            piece = back_out[b, low : low + segment]
            hit = jnp.where(rows_seg + (b * block + low) == at, piece, 0.0)
            sought = sought + jnp.sum(hit.reshape(segment // 8, 8, tracks), axis=0)
        found = jnp.where(rows8 == i, jnp.sum(sought, axis=0, keepdims=True), found)
    corner_out[...] = found
    corner_copy = remote(corner_out, corner_in, corner_send, corner_recv, below)
    corner_copy.start()
    back = [
        remote(back_out.at[b], back_in.at[b], back_send.at[b], back_recv.at[b], below) for b in range(faces)
    ]


    def step_upper(r, carry, now=now):
        upper[pl.ds(pl.multiple_of(r * block, block), block)] = relaxed(faces + r, now)
        return carry

    lax.fori_loop(0, faces, step_upper, 0, unroll=True)
    own = jnp.zeros((n_corners, tracks), jnp.float32)
    for i in range(n_corners):
        own = jnp.where(rows8 == i, upper[pl.ds(corners[0, i], 1)], own)

    all_of(0, n_line, columns, group_recv).wait()
    turned[...] = columns[...].reshape(n_line * n_corners, n_plane * n_corners).T

    corner_copy.wait_recv()
    at_corners = jnp.where(k < count - 1, corner_in[...], 0.0)
    totals[core, z] = own + at_corners
    over_z(1, lambda there: totals.at[core, z], totals.at[core])
    for copy in back:
        copy.start()
    own_jump = own - at_corners
    own_residual = jnp.zeros((n_corners, tracks), jnp.float32)
    for i in range(n_corners):
        own_residual = jnp.where(rows8 == i, residual[pl.ds(corners[0, i], 1)], own_residual)

    all_of(1, n_z, totals.at[core], group_recv).wait()
    to_sibling = remote(totals.at[core], totals.at[core], pair_send.at[0], pair_recv.at[0], sibling)
    to_sibling.start()
    to_sibling.wait_recv()
    part[...] = jnp.dot(
        turned[...],
        totals[...].reshape(n_line * n_corners, tracks),
        precision=lax.Precision.HIGHEST,
        preferred_element_type=jnp.float32,
    ).reshape(n_plane, n_corners, tracks)
    over_plane(2, lambda there: part.at[there], part_in)
    part_in[plane] = part[plane]

    for copy in back:
        copy.wait_recv()
    rows_in = lax.broadcasted_iota(jnp.int32, (rows32, tracks), 0)
    cross, curve = zero, zero
    for i in range(n_corners):
        for piece in range(segment // rows32):
            start = i * segment + piece * rows32
            v, low = start // block, start % block
            mapped = jnp.where(k < count - 1, back_in[back_at[v], low : low + rows32], 0.0)
            jump = upper[start : start + rows32] - mapped
            image[start : start + rows32] = jump
            jump = jnp.where(rows_in + start == corners[0, i], 0.0, jump)
            cross = add_product(cross, residual[start : start + rows32], jump)
            curve = add_product(curve, jump, jump)
    cross = fold((cross[0].reshape(4, 8, tracks), cross[1].reshape(4, 8, tracks)))
    curve = fold((curve[0].reshape(4, 8, tracks), curve[1].reshape(4, 8, tracks)))

    all_of(2, n_plane, part_in, group_recv).wait()
    coarse_part = jnp.sum(part_in[...], axis=0)
    at_nodes = own_jump + coarse_part
    cross = fold(tuple(v.reshape(n_corners, tracks) for v in add_product(cross, own_residual, at_nodes)))
    curve = fold(tuple(v.reshape(n_corners, tracks) for v in add_product(curve, at_nodes, at_nodes)))

    mine = jnp.concatenate([old[0], cross[0], curve[0], old[1], cross[1], curve[1]], axis=1)
    sums_plane[plane] = mine
    over_plane(3, lambda there: sums_plane.at[plane], sums_plane)
    for i in range(n_corners):
        for piece in range(segment // rows32):
            start = i * segment + piece * rows32
            added = jnp.where(rows_in + start == corners[0, i], coarse_part[i : i + 1], 0.0)
            image[start : start + rows32] = image[start : start + rows32] + added

    store = pltpu.make_async_copy(image, image_hbm, load_sem.at[0])
    store.start()

    def total_of(buffer):
        pair = fold((buffer[:, :, : 3 * tracks], buffer[:, :, 3 * tracks :]))
        return tuple(v.reshape(1, 3 * tracks) for v in tidy(pair))

    all_of(3, n_plane, sums_plane, group_recv).wait()
    sums_line[z] = jnp.concatenate(total_of(sums_plane), axis=1)
    over_z(4, lambda there: sums_line.at[z], sums_line)
    all_of(4, n_z, sums_line, group_recv).wait()
    sums_pair[core] = jnp.concatenate(total_of(sums_line), axis=1)
    sums_to_sibling = remote(sums_pair.at[core], sums_pair.at[core], pair_send.at[1], pair_recv.at[1], sibling)
    sums_to_sibling.start()
    sums_to_sibling.wait_recv()
    pair = total_of(sums_pair)
    old, cross, curve = (
        tuple(v[:, i * tracks : (i + 1) * tracks] for v in pair) for i in range(3)
    )
    length = cross[0] / curve[0]
    scale = 2.0**-14
    old, cross, curve = (tuple(v * scale for v in pair) for pair in (old, cross, curve))
    inner, inner_low = two_product(-length, curve[0])
    inner = tidy(pair_add((2.0 * cross[0], 2.0 * cross[1]), (inner, inner_low - length * curve[1])))
    outer, outer_low = two_product(-length, inner[0])
    new = tidy(pair_add(old, (outer, outer_low - length * inner[1])))
    factors[0:1] = length
    factors[1:2] = jnp.maximum(new[0], 0.0) / old[0]

    store.wait()
    for copy in forward + back + [corner_copy, to_sibling, sums_to_sibling]:
        copy.wait_send()
    for stage, (size, buffer) in enumerate(
        ((n_line, columns), (n_z, totals.at[0]), (n_plane, part_in), (n_plane, sums_plane), (n_z, sums_line))
    ):
        all_of(stage, size, buffer, group_send).wait()


def per_device(sizes, residual, direction, sub_blocks, pattern, facing, corners, coarse_inverse):
    n_z, n_yl, n_grp, n_rep = sizes
    n_line, n_plane = n_z * CORES, n_yl * n_grp * n_rep
    face_rows, tracks = residual.shape
    row_blocks, nnz, block, _ = sub_blocks.shape
    faces, n_corners = facing.shape[1], corners.shape[1]
    f32, vmem, smem = jnp.float32, pltpu.VMEM, pltpu.SMEM
    dma = pltpu.SemaphoreType.DMA
    image, factors = pl.pallas_call(
        functools.partial(kernel, sizes),
        out_shape=(jax.ShapeDtypeStruct((face_rows, tracks), f32), jax.ShapeDtypeStruct((2, tracks), f32)),
        in_specs=[pl.BlockSpec(memory_space=pltpu.HBM)] * 7,
        out_specs=(pl.BlockSpec(memory_space=pl.ANY), pl.BlockSpec(memory_space=vmem)),
        scratch_shapes=[
            smem((nnz, row_blocks), jnp.int32),
            smem(facing.shape, jnp.int32),
            smem(corners.shape, jnp.int32),
            vmem((face_rows, tracks), f32),
            vmem((face_rows, tracks), f32),
            vmem((faces, block, tracks), f32),
            vmem(sub_blocks.shape, sub_blocks.dtype),
            vmem(coarse_inverse.shape, f32),
            vmem((row_blocks, block, tracks), f32),
            vmem((row_blocks, block, tracks), jnp.bfloat16),
            vmem((row_blocks, block, tracks), jnp.bfloat16),
            vmem((face_rows, tracks), f32),
            vmem((faces, block + n_corners, tracks), f32),
            vmem((faces, block + n_corners, tracks), f32),
            vmem((faces, block, tracks), f32),
            vmem((faces, block, tracks), f32),
            vmem((n_corners, tracks), f32),
            vmem((n_corners, tracks), f32),
            vmem((n_line, n_corners, n_plane * n_corners), f32),
            vmem((n_line, n_corners, n_plane * n_corners), f32),
            vmem((n_plane * n_corners, n_line * n_corners), f32),
            vmem((CORES, n_z, n_corners, tracks), f32),
            vmem((n_plane, n_corners, tracks), f32),
            vmem((n_plane, n_corners, tracks), f32),
            vmem((n_plane, 1, 6 * tracks), f32),
            vmem((n_z, 1, 6 * tracks), f32),
            vmem((CORES, 1, 6 * tracks), f32),
            dma((7,)),
            dma((faces,)),
            dma((faces,)),
            dma((faces,)),
            dma((faces,)),
            dma,
            dma,
            dma((5,)),
            dma((5,)),
            dma((2,)),
            dma((2,)),
        ],
        compiler_params=pltpu.CompilerParams(
            collective_id=0, has_side_effects=True, vmem_limit_bytes=62 * 1024 * 1024
        ),
    )(
        pattern.T,
        facing,
        corners,
        residual,
        direction.reshape(faces, block, tracks),
        sub_blocks,
        coarse_inverse,
    )
    residual_new = residual - factors[0:1] * image
    return residual_new, residual_new + factors[1:2] * direction


def solution(mesh):
    n_sub, n_grp, n_rep = (mesh.shape[a] for a in AXES)
    n_yl = 4 if n_sub % (4 * CORES) == 0 else 2
    sizes = (n_sub // (n_yl * CORES), n_yl, n_grp, n_rep)
    rows = P(AXES, None)
    return jax.shard_map(
        functools.partial(per_device, sizes),
        mesh=mesh,
        in_specs=(rows, rows, P(AXES, None, None, None), rows, rows, rows, rows),
        out_specs=(rows, rows),
        check_vma=False,
    )
```

```python
import functools

import jax
import jax.numpy as jnp
from jax import lax
from jax.experimental import pallas as pl
from jax.experimental.pallas import tpu as pltpu
from jax.sharding import PartitionSpec as P

MESH = pl.DeviceIdType.MESH
AXES = ("sub", "grp", "rep")
SWEEPS = 3
CORES = 2
LANES = 128


def two_sum(a, b):
    s = a + b
    t = s - a
    return s, (a - (s - t)) + (b - t)


def split(a):
    c = a * 4097.0
    hi = c - (c - a)
    return hi, a - hi


def two_product(a, b):
    p = a * b
    ah, al = split(a)
    bh, bl = split(b)
    return p, ((ah * bh - p) + ah * bl + al * bh) + al * bl


def pair_add(a, b):
    s, e = two_sum(a[0], b[0])
    return s, e + (a[1] + b[1])


def tidy(a):
    s = a[0] + a[1]
    return s, a[1] - (s - a[0])


def add_product(total, a, b):
    p, e = two_product(a, b)
    return pair_add(total, (p, e))


def fold(pair, axis=0):
    while pair[0].shape[axis] > 1:
        half = pair[0].shape[axis] // 2
        pair = pair_add(
            tuple(lax.slice_in_dim(v, 0, half, axis=axis) for v in pair),
            tuple(lax.slice_in_dim(v, half, 2 * half, axis=axis) for v in pair),
        )
    return pair


def kernel(
    sizes,
    pattern_hbm,
    facing_hbm,
    corners_hbm,
    residual_hbm,
    direction_hbm,
    blocks_hbm,
    coarse_hbm,
    image_hbm,
    factors,
    pattern,
    facing,
    corners,
    image,
    residual,
    direction,
    blocks,
    coarse,
    source,
    rounded,
    rounded_next,
    upper,
    forward_out,
    forward_in,
    back_out,
    back_in,
    corner_out,
    corner_in,
    packed,
    columns,
    turned,
    totals,
    part,
    part_in,
    sums_plane,
    sums_line,
    sums_pair,
    load_sem,
    forward_send,
    forward_recv,
    back_send,
    back_recv,
    corner_send,
    corner_recv,
    group_send,
    group_recv,
    pair_send,
    pair_recv,
):
    n_z, n_yl, n_grp, n_rep = sizes
    n_line, n_plane = n_z * CORES, n_yl * n_grp * n_rep
    count = n_line * n_plane
    faces, block, tracks = forward_in.shape[0], direction.shape[1], direction.shape[2]
    row_blocks, nnz = blocks.shape[:2]
    n_corners = corners.shape[1]
    segment = faces * block // n_corners
    per_block = block // segment

    sub, grp, rep = (lax.axis_index(a) for a in AXES)
    k = (sub * n_grp + grp) * n_rep + rep
    core, yl, z = sub % CORES, (sub // CORES) % n_yl, sub // (CORES * n_yl)
    line = core * n_z + z
    plane = (yl * n_grp + grp) * n_rep + rep

    def device_of(index):
        return (index // (n_grp * n_rep), (index // n_rep) % n_grp, index % n_rep)

    def ring(step, size):
        return min(step, size - step)

    z_steps = sorted(range(1, n_z), key=lambda step: -ring(step, n_z))

    def plane_hops(step):
        over_y = ring(step // (n_grp * n_rep), n_yl)
        if step % n_rep:
            over_y = n_yl - over_y
        return over_y + ring(step // n_rep % n_grp, n_grp)

    plane_steps = sorted(range(1, n_plane), key=lambda step: -plane_hops(step))

    def plane_at(step):
        there_yl = (yl + step // (n_grp * n_rep)) % n_yl
        there_grp = (grp + step // n_rep % n_grp) % n_grp
        return (there_yl * n_grp + there_grp) * n_rep + (rep + step) % n_rep

    def on_line(place):
        return ((place % n_z * n_yl + yl) * CORES + place // n_z, grp, rep)

    def on_plane(place):
        there = (z * n_yl + place // (n_grp * n_rep)) * CORES + core
        return (there, (place // n_rep) % n_grp, place % n_rep)

    def along_z(place):
        return ((place * n_yl + yl) * CORES + core, grp, rep)

    sibling = ((z * n_yl + yl) * CORES + 1 - core, grp, rep)
    above, below = device_of((k + 1) % count), device_of((k + count - 1) % count)

    barrier = pltpu.get_barrier_semaphore()

    def greet(device):
        pl.semaphore_signal(barrier, inc=1, device_id=device, device_id_type=MESH)

    greet(above)
    greet(below)
    for step in z_steps:
        for other in range(CORES):
            greet((((z + step) % n_z * n_yl + yl) * CORES + other, grp, rep))
    for step in plane_steps:
        greet(on_plane(plane_at(step)))
    greet(sibling)

    loads = [
        pltpu.make_async_copy(a, b, load_sem.at[i])
        for i, (a, b) in enumerate(
            (
                (facing_hbm, facing),
                (corners_hbm, corners),
                (direction_hbm, direction),
                (coarse_hbm, coarse),
                (residual_hbm, residual),
                (pattern_hbm, pattern),
                (blocks_hbm, blocks),
            )
        )
    ]
    for load in loads:
        load.start()
    for load in loads[:3]:
        load.wait()

    back_at = []
    for v in range(faces):
        place = jnp.int32(0)
        for b in range(faces):
            place = jnp.where(facing[0, b] == v, b, place)
        back_at.append(place)

    for b in range(faces):
        forward_out[b, :block] = direction[facing[0, b]]
    rows8 = lax.broadcasted_iota(jnp.int32, (n_corners, tracks), 0)
    wanted = jnp.zeros((n_corners, tracks), jnp.int32)
    for i in range(n_corners):
        wanted = jnp.where(rows8 == i, back_at[i // per_block] * block + corners[0, i] % block, wanted)
    forward_out[faces - 1, block:] = wanted.astype(jnp.float32)

    loads[3].wait()
    lanes = lax.broadcasted_iota(jnp.int32, (n_corners, LANES), 1)
    half = LANES // CORES
    for zz in range(n_z):
        for q in range(n_yl // CORES):
            first = coarse[:, pl.ds((zz * n_yl + 2 * q) * LANES, LANES)]
            second = coarse[:, pl.ds((zz * n_yl + 2 * q + 1) * LANES, LANES)]
            at = pl.ds(q * LANES, LANES)
            packed[zz, :, at] = jnp.where(lanes < half, first, pltpu.roll(second, half, 1))
            packed[n_z + zz, :, at] = jnp.where(lanes < half, pltpu.roll(first, half, 1), second)

    pl.semaphore_wait(barrier, n_line + n_plane)

    def remote(source_ref, target_ref, send, recv, device):
        return pltpu.make_async_remote_copy(
            src_ref=source_ref,
            dst_ref=target_ref,
            send_sem=send,
            recv_sem=recv,
            device_id=device,
            device_id_type=MESH,
        )

    forward = []
    for b in range(faces):
        rows = pl.ds(0, block if b < faces - 1 else block + n_corners)
        forward.append(
            remote(forward_out.at[b, rows], forward_in.at[b, rows], forward_send.at[b], forward_recv.at[b], above)
        )
        forward[-1].start()

    def exchange(stage, size, mine, where, source_of, target):
        @pl.loop(1, size)
        def _(j):
            there = (mine + j) % size
            remote(
                source_of(there), target.at[mine], group_send.at[stage], group_recv.at[stage], where(there)
            ).start()

    def send_all(stage, places, where, mine, source_of, target):
        for there in places:
            remote(
                source_of(there), target.at[mine], group_send.at[stage], group_recv.at[stage], where(there)
            ).start()

    def over_z(stage, source_of, target):
        send_all(stage, [(z + step) % n_z for step in z_steps], along_z, z, source_of, target)

    def over_plane(stage, source_of, target):
        send_all(stage, [plane_at(step) for step in plane_steps], on_plane, plane, source_of, target)

    def all_of(stage, size, target, sems):
        rest = target.at[pl.ds(0, size - 1)]
        return pltpu.make_async_copy(rest, rest, sems.at[stage])

    exchange(0, n_line, line, on_line, lambda there: packed.at[there], columns)
    columns[line] = packed[line]

    rows32 = 32
    zero = (jnp.zeros((rows32, tracks), jnp.float32),) * 2
    loads[4].wait()

    def add_old(i, total):
        r = residual[pl.ds(pl.multiple_of(i * rows32, rows32), rows32)]
        return add_product(total, r, r)

    old = fold(lax.fori_loop(0, faces * block // rows32, add_old, zero))
    for r in range(2 * faces, row_blocks):
        source[r] = jnp.zeros((block, tracks), jnp.float32)
        rounded[r] = jnp.zeros((block, tracks), rounded.dtype)
    for b in range(faces):
        source[faces + b] = direction[b]
        rounded[faces + b] = direction[b].astype(rounded.dtype)
    loads[5].wait()
    loads[6].wait()
    for b in range(faces):
        forward[b].wait_recv()
        arrived = jnp.where(k > 0, -forward_in[b, :block], 0.0)
        source[b] = arrived
        rounded[b] = arrived.astype(rounded.dtype)

    def relaxed(r, now):
        left = jnp.concatenate([blocks[r, j] for j in range(nnz)], axis=1)
        right = jnp.concatenate([now[pattern[j, r]] for j in range(nnz)], axis=0)
        return source[r] - jnp.dot(left, right, preferred_element_type=jnp.float32)

    now, later = rounded, rounded_next
    for _ in range(SWEEPS - 1):

        def step(r, carry, now=now, later=later):
            later[r] = relaxed(r, now).astype(later.dtype)
            return carry

        lax.fori_loop(0, row_blocks, step, 0, unroll=True)
        now, later = later, now

    def step_lower(r, carry, now=now):
        back_out[r] = relaxed(r, now)
        return carry

    lax.fori_loop(0, faces, step_lower, 0, unroll=True)

    rows_seg = lax.broadcasted_iota(jnp.int32, (segment, tracks), 0)
    found = jnp.zeros((n_corners, tracks), jnp.float32)
    for i in range(n_corners):
        at = forward_in[faces - 1, block + i : block + i + 1].astype(jnp.int32)
        low = (i % per_block) * segment
        sought = jnp.zeros((8, tracks), jnp.float32)
        for b in range(faces):
            piece = back_out[b, low : low + segment]
            hit = jnp.where(rows_seg + (b * block + low) == at, piece, 0.0)
            sought = sought + jnp.sum(hit.reshape(segment // 8, 8, tracks), axis=0)
        found = jnp.where(rows8 == i, jnp.sum(sought, axis=0, keepdims=True), found)
    corner_out[...] = found
    corner_copy = remote(corner_out, corner_in, corner_send, corner_recv, below)
    corner_copy.start()
    back = [
        remote(back_out.at[b], back_in.at[b], back_send.at[b], back_recv.at[b], below) for b in range(faces)
    ]


    def step_upper(r, carry, now=now):
        upper[pl.ds(pl.multiple_of(r * block, block), block)] = relaxed(faces + r, now)
        return carry

    lax.fori_loop(0, faces, step_upper, 0, unroll=True)
    own = jnp.zeros((n_corners, tracks), jnp.float32)
    for i in range(n_corners):
        own = jnp.where(rows8 == i, upper[pl.ds(corners[0, i], 1)], own)


    corner_copy.wait_recv()
    at_corners = jnp.where(k < count - 1, corner_in[...], 0.0)
    totals[core, z] = own + at_corners
    over_z(1, lambda there: totals.at[core, z], totals.at[core])
    for copy in back:
        copy.start()
    own_jump = own - at_corners
    own_residual = jnp.zeros((n_corners, tracks), jnp.float32)
    for i in range(n_corners):
        own_residual = jnp.where(rows8 == i, residual[pl.ds(corners[0, i], 1)], own_residual)

    all_of(0, n_line, columns, group_recv).wait()
    turned[...] = columns[...].reshape(n_line * n_corners, n_plane * n_corners).T
    all_of(1, n_z, totals.at[core], group_recv).wait()
    to_sibling = remote(totals.at[core], totals.at[core], pair_send.at[0], pair_recv.at[0], sibling)
    to_sibling.start()
    to_sibling.wait_recv()
    part[...] = jnp.dot(
        turned[...],
        totals[...].reshape(n_line * n_corners, tracks),
        precision=lax.Precision.HIGHEST,
        preferred_element_type=jnp.float32,
    ).reshape(n_plane, n_corners, tracks)
    over_plane(2, lambda there: part.at[there], part_in)
    part_in[plane] = part[plane]

    for copy in back:
        copy.wait_recv()
    rows_in = lax.broadcasted_iota(jnp.int32, (rows32, tracks), 0)
    cross, curve = zero, zero
    for i in range(n_corners):
        for piece in range(segment // rows32):
            start = i * segment + piece * rows32
            v, low = start // block, start % block
            mapped = jnp.where(k < count - 1, back_in[back_at[v], low : low + rows32], 0.0)
            jump = upper[start : start + rows32] - mapped
            image[start : start + rows32] = jump
            jump = jnp.where(rows_in + start == corners[0, i], 0.0, jump)
            cross = add_product(cross, residual[start : start + rows32], jump)
            curve = add_product(curve, jump, jump)
    cross = fold((cross[0].reshape(4, 8, tracks), cross[1].reshape(4, 8, tracks)))
    curve = fold((curve[0].reshape(4, 8, tracks), curve[1].reshape(4, 8, tracks)))

    all_of(2, n_plane, part_in, group_recv).wait()
    coarse_part = jnp.sum(part_in[...], axis=0)
    at_nodes = own_jump + coarse_part
    cross = fold(tuple(v.reshape(n_corners, tracks) for v in add_product(cross, own_residual, at_nodes)))
    curve = fold(tuple(v.reshape(n_corners, tracks) for v in add_product(curve, at_nodes, at_nodes)))

    mine = jnp.concatenate([old[0], cross[0], curve[0], old[1], cross[1], curve[1]], axis=1)
    sums_plane[plane] = mine
    over_plane(3, lambda there: sums_plane.at[plane], sums_plane)
    for i in range(n_corners):
        for piece in range(segment // rows32):
            start = i * segment + piece * rows32
            added = jnp.where(rows_in + start == corners[0, i], coarse_part[i : i + 1], 0.0)
            image[start : start + rows32] = image[start : start + rows32] + added

    store = pltpu.make_async_copy(image, image_hbm, load_sem.at[0])
    store.start()

    def total_of(buffer):
        pair = fold((buffer[:, :, : 3 * tracks], buffer[:, :, 3 * tracks :]))
        return tuple(v.reshape(1, 3 * tracks) for v in tidy(pair))

    all_of(3, n_plane, sums_plane, group_recv).wait()
    sums_line[z] = jnp.concatenate(total_of(sums_plane), axis=1)
    over_z(4, lambda there: sums_line.at[z], sums_line)
    all_of(4, n_z, sums_line, group_recv).wait()
    sums_pair[core] = jnp.concatenate(total_of(sums_line), axis=1)
    sums_to_sibling = remote(sums_pair.at[core], sums_pair.at[core], pair_send.at[1], pair_recv.at[1], sibling)
    sums_to_sibling.start()
    sums_to_sibling.wait_recv()
    pair = total_of(sums_pair)
    old, cross, curve = (
        tuple(v[:, i * tracks : (i + 1) * tracks] for v in pair) for i in range(3)
    )
    length = cross[0] / curve[0]
    scale = 2.0**-14
    old, cross, curve = (tuple(v * scale for v in pair) for pair in (old, cross, curve))
    inner, inner_low = two_product(-length, curve[0])
    inner = tidy(pair_add((2.0 * cross[0], 2.0 * cross[1]), (inner, inner_low - length * curve[1])))
    outer, outer_low = two_product(-length, inner[0])
    new = tidy(pair_add(old, (outer, outer_low - length * inner[1])))
    factors[0:1] = length
    factors[1:2] = jnp.maximum(new[0], 0.0) / old[0]

    store.wait()
    for copy in forward + back + [corner_copy, to_sibling, sums_to_sibling]:
        copy.wait_send()
    for stage, (size, buffer) in enumerate(
        ((n_line, columns), (n_z, totals.at[0]), (n_plane, part_in), (n_plane, sums_plane), (n_z, sums_line))
    ):
        all_of(stage, size, buffer, group_send).wait()


def per_device(sizes, residual, direction, sub_blocks, pattern, facing, corners, coarse_inverse):
    n_z, n_yl, n_grp, n_rep = sizes
    n_line, n_plane = n_z * CORES, n_yl * n_grp * n_rep
    face_rows, tracks = residual.shape
    row_blocks, nnz, block, _ = sub_blocks.shape
    faces, n_corners = facing.shape[1], corners.shape[1]
    f32, vmem, smem = jnp.float32, pltpu.VMEM, pltpu.SMEM
    dma = pltpu.SemaphoreType.DMA
    image, factors = pl.pallas_call(
        functools.partial(kernel, sizes),
        out_shape=(jax.ShapeDtypeStruct((face_rows, tracks), f32), jax.ShapeDtypeStruct((2, tracks), f32)),
        in_specs=[pl.BlockSpec(memory_space=pltpu.HBM)] * 7,
        out_specs=(pl.BlockSpec(memory_space=pl.ANY), pl.BlockSpec(memory_space=vmem)),
        scratch_shapes=[
            smem((nnz, row_blocks), jnp.int32),
            smem(facing.shape, jnp.int32),
            smem(corners.shape, jnp.int32),
            vmem((face_rows, tracks), f32),
            vmem((face_rows, tracks), f32),
            vmem((faces, block, tracks), f32),
            vmem(sub_blocks.shape, sub_blocks.dtype),
            vmem(coarse_inverse.shape, f32),
            vmem((row_blocks, block, tracks), f32),
            vmem((row_blocks, block, tracks), jnp.bfloat16),
            vmem((row_blocks, block, tracks), jnp.bfloat16),
            vmem((face_rows, tracks), f32),
            vmem((faces, block + n_corners, tracks), f32),
            vmem((faces, block + n_corners, tracks), f32),
            vmem((faces, block, tracks), f32),
            vmem((faces, block, tracks), f32),
            vmem((n_corners, tracks), f32),
            vmem((n_corners, tracks), f32),
            vmem((n_line, n_corners, n_plane * n_corners), f32),
            vmem((n_line, n_corners, n_plane * n_corners), f32),
            vmem((n_plane * n_corners, n_line * n_corners), f32),
            vmem((CORES, n_z, n_corners, tracks), f32),
            vmem((n_plane, n_corners, tracks), f32),
            vmem((n_plane, n_corners, tracks), f32),
            vmem((n_plane, 1, 6 * tracks), f32),
            vmem((n_z, 1, 6 * tracks), f32),
            vmem((CORES, 1, 6 * tracks), f32),
            dma((7,)),
            dma((faces,)),
            dma((faces,)),
            dma((faces,)),
            dma((faces,)),
            dma,
            dma,
            dma((5,)),
            dma((5,)),
            dma((2,)),
            dma((2,)),
        ],
        compiler_params=pltpu.CompilerParams(
            collective_id=0, has_side_effects=True, vmem_limit_bytes=62 * 1024 * 1024
        ),
    )(
        pattern.T,
        facing,
        corners,
        residual,
        direction.reshape(faces, block, tracks),
        sub_blocks,
        coarse_inverse,
    )
    residual_new = residual - factors[0:1] * image
    return residual_new, residual_new + factors[1:2] * direction


def solution(mesh):
    n_sub, n_grp, n_rep = (mesh.shape[a] for a in AXES)
    n_yl = 4 if n_sub % (4 * CORES) == 0 else 2
    sizes = (n_sub // (n_yl * CORES), n_yl, n_grp, n_rep)
    rows = P(AXES, None)
    return jax.shard_map(
        functools.partial(per_device, sizes),
        mesh=mesh,
        in_specs=(rows, rows, P(AXES, None, None, None), rows, rows, rows, rows),
        out_specs=(rows, rows),
        check_vma=False,
    )
```
